512 devices in a mesh: rows: 128 (over y_lo, z, x, core), feat: 4 (over y_hi).
Axes of the slice: x: 4, y: 8 (y_hi: 4, y_lo: 2; y = y_hi * 2 + y_lo), z: 8, core: 2. Of those that a mesh axis runs over, the one named last changes fastest.
Arguments:
- train_grads: bfloat16 [131072, 2048], P('rows', 'feat'), may hold values from -50 to 50, as said below
- test_feats: bfloat16 [1024, 2048], P(None, 'feat'), may hold values from -6 to 6
Outputs:
- scores: bfloat16 [131072, 1024], P('rows', 'feat')
- gram: float32 [2048, 2048], P('rows', 'feat')
The draws below stay inside these ranges and needn't reach their ends.
Inputs may be any that keep to these rules, and one draw needn't show every extreme that they name: `train_grads`: projected gradients of moderate size.
All inputs are finite; a program needn't handle non-finite values.
Results may differ from the reference program's by a relative error of at most 0.00055.
Values may be sent and summed in bfloat16 or wider, within the bound.
No kernel may reach another device: no remote copies, remote signals or barrier semaphores. Data moves between devices by JAX's collectives and lax.ppermute only.
A program may use at most 64 MiB of HBM per device.

```python
import math
import jax
import jax.numpy as jnp
from jax import lax

K = 2048
NTEST = 1024
R_DEV = 1024
NTRAIN = 131072


def draw_train_grads(key, part):
    key = jax.random.fold_in(key, 11)
    first_key, second_key, third_key = jax.random.split(key, 3)
    blocks = NTRAIN // R_DEV
    block_means = 2.0 * jnp.clip(jax.random.normal(second_key, (blocks, K), jnp.float32), -4.0, 4.0)
    jitter_vals = jnp.clip(jax.random.normal(first_key, (NTRAIN, K), jnp.float32), -5.0, 5.0)
    row_scale = jnp.exp(jax.random.uniform(third_key, (NTRAIN, 1), jnp.float32, math.log(0.5), math.log(2.0)))
    values = row_scale * (jitter_vals + jnp.repeat(block_means, R_DEV, axis=0))
    return values.astype(jnp.bfloat16)


def block_scale(key, dims, cuts, least, top_value):
    def one(axis_at, parts):
        draws = jax.random.uniform(jax.random.fold_in(jax.random.fold_in(key, 6), axis_at), (parts,), jnp.float32, least / len(cuts), top_value / len(cuts))
        return jnp.repeat(jnp.exp(draws), dims[axis_at] // parts).reshape((-1,) + (1,) * (len(dims) - axis_at - 1))

    factor_of = one(*cuts[0])
    for cut in cuts[1:]:
        factor_of = factor_of * one(*cut)
    return factor_of


def normal_values(rng, extent, width, reach, cuts=(), kind=jnp.bfloat16):
    loudness = block_scale(rng, extent, cuts, -0.22, 0.18) if cuts else 1.0
    result = jax.random.normal(rng, extent, jnp.float32) * width * loudness
    return jnp.minimum(jnp.maximum(result, -reach), reach).astype(kind)


def setup_inputs(seed: int = 0) -> dict:
    key_list = jax.random.split(jax.random.key(seed), 3)
    return {
        "train_grads": draw_train_grads(jax.random.fold_in(key_list[2], 71), 0),
        "test_feats": normal_values(key_list[1], (NTEST, K), 1.0, 6.0, ((1, 4),)),
    }


def reference(train_grads, test_feats):
    queries = test_feats.astype(jnp.float32)
    row_blocks = train_grads.reshape(NTRAIN // R_DEV, R_DEV, K)

    def absorb(gram_acc, block_rows):
        block_float = block_rows.astype(jnp.float32)
        gram_acc = gram_acc + lax.dot_general(block_float, block_float, (((0,), (0,)), ((), ())), precision=lax.Precision.HIGHEST, preferred_element_type=jnp.float32)
        raw_scores = lax.dot_general(block_float, queries, (((1,), (1,)), ((), ())), precision=lax.Precision.HIGHEST, preferred_element_type=jnp.float32)
        return gram_acc, (raw_scores * (K ** -0.5)).astype(jnp.bfloat16)

    gram_acc, score_blocks = lax.scan(absorb, jnp.zeros((K, K), jnp.float32), row_blocks)
    return score_blocks.reshape(NTRAIN, NTEST), gram_acc / NTRAIN
```

```python
import jax
import jax.numpy as jnp
from jax import lax
from jax.sharding import Mesh, PartitionSpec as P

NF = 4
F16_SCALE = 2.0**-7


def dot(a, b, dims):
    return lax.dot_general(a, b, (dims, ((), ())), preferred_element_type=jnp.float32)


def body(train_grads, test_feats):
    rows, width = train_grads.shape
    f, core = lax.axis_index("feat"), lax.axis_index("core")
    group = lax.axis_index(("ylo", "zhi"))
    up = [(i, (i + 1) % NF) for i in range(NF)]
    down = [(i, (i - 1) % NF) for i in range(NF)]

    before = lax.ppermute(train_grads, "feat", up)
    after = lax.ppermute(train_grads, "feat", down)

    tests = test_feats.shape[0] // NF
    lot = lax.axis_index(("zhi", "zlo", "x"))
    mine = lax.dynamic_index_in_dim(test_feats.reshape(NF, 32, tests // 32, width), lot, 1, keepdims=False)
    mine = lax.all_to_all(mine, "feat", split_axis=0, concat_axis=0, tiled=True)
    shared = jnp.broadcast_to(mine[None], (32,) + mine.shape)
    shared = lax.all_to_all(shared, ("zhi", "zlo", "x"), split_axis=0, concat_axis=0, tiled=True)
    queries = shared.transpose(1, 0, 2, 3).reshape(NF, tests, width)

    def query(k):
        return lax.dynamic_index_in_dim(queries, (f + k) % NF, 0, keepdims=False)

    half = rows // 2
    far_top = lax.ppermute(before[:half], "feat", up)
    far_bottom = lax.ppermute(after[half:], "feat", down)

    pairs = ((train_grads, train_grads), (after, train_grads), (after, before), (before, train_grads))
    terms = [dot(a, b, ((0,), (0,))) for a, b in pairs]
    terms = jnp.stack([t.reshape(16, 2, 16, width) for t in terms])

    def half_of(c):
        part = lax.dynamic_index_in_dim(terms, c, 2, keepdims=False)
        return jnp.roll(part, f, axis=0)

    sent = (half_of(1 - core) * F16_SCALE).astype(jnp.float16)
    got = lax.ppermute(sent, "core", [(0, 1), (1, 0)])
    both = half_of(core) * F16_SCALE + got.astype(jnp.float32)
    lots = both.astype(jnp.float16).reshape(64, 16, width)
    lots = lax.all_to_all(lots, ("ylo", "zhi", "zlo", "x"), split_axis=0, concat_axis=0, tiled=True)
    train_count = rows * 128
    summed = jnp.sum(lots.astype(jnp.float32), axis=0) * (1.0 / F16_SCALE / train_count)
    moves = [(((i + 2) % NF) * NF + i, ((i + 1) % NF) * NF + (i - 1) % NF) for i in range(NF)]
    moved = lax.ppermute(summed, ("ylo", "zhi", "feat"), moves)
    gram = jnp.where(group == (f + 2) % NF, moved, summed)

    on_features = ((1,), (1,))
    raw = dot(train_grads, query(0), on_features) + dot(before, query(3), on_features) + dot(after, query(1), on_features)
    far = jnp.concatenate([far_top, far_bottom])
    raw = raw + dot(far, query(2), on_features)
    scores = (raw * (NF * width) ** (-0.5)).astype(jnp.bfloat16)
    return (scores, gram)


def solution(mesh):
    fine = Mesh(mesh.devices.reshape(2, 2, 4, 4, 2, 4), ("ylo", "zhi", "zlo", "x", "core", "feat"))
    split = ("ylo", "zhi", "zlo", "x", "core")
    in_specs = (P(split, "feat"), P(None, "feat"))
    out_specs = (P(split, "feat"), P(split, "feat"))
    return jax.shard_map(body, mesh=fine, in_specs=in_specs, out_specs=out_specs, check_vma=False)
```

```python
import jax
import jax.numpy as jnp
from jax import lax
from jax.experimental import pallas as pl
from jax.experimental.pallas import tpu as pltpu
from jax.sharding import Mesh, PartitionSpec as P

NF = 4
NEAR_FLOPS = 0
WIDE_FLOPS = 1 << 36
SCORE_FLOPS = 68719476736
SCORE_BYTES = 1073741824
F16_SCALE = 2.0**-7
AXES = ("ylo", "zhi", "zlo", "x", "core", "feat")


def dot(a, b, on):
    return lax.dot_general(a, b, (((on,), (on,)), ((), ())), preferred_element_type=jnp.float32)


def store_unit(place, product, keep, send):
    parts = product.reshape(16, 16, product.shape[1])
    low, high = parts[:, :8], parts[:, 8:]
    first = place[1] == 0
    keep[0] = jnp.where(first, low, high)
    send[0] = jnp.where(first, high, low)


def near_kernel(place, own, before0, after0, keep, send):
    half = before0.shape[1]
    lefts = (
        lambda: own[:, :half],
        lambda: own[:, half:],
        lambda: before0[...],
        lambda: after0[...],
    )
    for k, left in enumerate(lefts):

        @pl.when(pl.program_id(0) == k)
        def _():
            store_unit(place, dot(left(), own[...], 0), keep, send)


def wide_kernel(place, own, before0, before1, after0, after1, earlier, keep, send):
    del earlier
    for k, left in enumerate((before1, after1)):

        @pl.when(pl.program_id(0) == k)
        def _():
            store_unit(place, dot(left[...], own[...], 0), keep, send)

    for k, left in enumerate((after0, after1)):

        @pl.when(pl.program_id(0) == k + 2)
        def _():
            across = jnp.concatenate([dot(left[...], before0[...], 0), dot(left[...], before1[...], 0)], axis=1)
            store_unit(place, across, keep, send)


def gram_units(kernel, place, blocks, flops, earlier=()):
    rows, width = blocks[0].shape
    unit = pl.BlockSpec((1, 16, 8, width), lambda k, place: ((place[0] + k) % NF, 0, 0, 0))
    shape = jax.ShapeDtypeStruct((NF, 16, 8, width), jnp.float32)
    return pl.pallas_call(
        kernel,
        out_shape=(shape, shape),
        grid_spec=pltpu.PrefetchScalarGridSpec(
            num_scalar_prefetch=1,
            grid=(NF,),
            in_specs=[pl.BlockSpec(b.shape, lambda k, place: (0, 0)) for b in blocks]
            + [pl.BlockSpec(memory_space=pl.ANY) for _ in earlier],
            out_specs=(unit, unit),
        ),
        compiler_params=pltpu.CompilerParams(vmem_limit_bytes=40 << 20),
        cost_estimate=pl.CostEstimate(flops=flops, bytes_accessed=flops, transcendentals=0),
    )(place, *blocks, *earlier)


def scores_kernel(own, before0, before1, after0, after1, far0, far1, queries, scores):
    half = before0.shape[1]
    total = dot(own[...], queries[0], 1)
    for k, first, second in ((1, after0, after1), (2, far0, far1), (3, before0, before1)):
        asked = queries[k]
        total += dot(first[...], asked[:, :half], 1) + dot(second[...], asked[:, half:], 1)
    scores[...] = (total * (2 * half * NF) ** (-0.5)).astype(scores.dtype)


def score_rows(blocks, queries):
    rows, tests = blocks[0].shape[0], queries.shape[1]
    step = 256
    return pl.pallas_call(
        scores_kernel,
        out_shape=jax.ShapeDtypeStruct((rows, tests), jnp.bfloat16),
        grid=(rows // step,),
        in_specs=[pl.BlockSpec((step, b.shape[1]), lambda i: (i, 0)) for b in blocks]
        + [pl.BlockSpec(queries.shape, lambda i: (0, 0, 0))],
        out_specs=pl.BlockSpec((step, tests), lambda i: (i, 0)),
        compiler_params=pltpu.CompilerParams(vmem_limit_bytes=40 << 20),
        cost_estimate=pl.CostEstimate(flops=SCORE_FLOPS, bytes_accessed=SCORE_BYTES, transcendentals=0),
    )(*blocks, queries)


def chip_sum(keep, send, other=None):
    if other is not None:
        send, other = lax.optimization_barrier((send, other))
    got = lax.ppermute(send, "core", [(0, 1), (1, 0)])
    return ((keep + got) * F16_SCALE).astype(jnp.float16), got


def slice_sum(lots, other=None):
    rows, width = lots.shape[-2:]
    lots = lax.all_to_all(lots.reshape(64, rows, width), AXES[:4], split_axis=0, concat_axis=0, tiled=True)
    if other is not None:
        lots, other = lax.optimization_barrier((lots, other))
    return jnp.sum(lots.astype(jnp.float32), axis=0)


def final_moves():
    first, second = [], []
    for source in range(512):
        f, c, w, g = source % 4, source // 4 % 2, source // 8 % 16, source // 128
        k = (g - f) % NF
        near = ((f, 0, f), (f, 1, f), (f - 1, 0, f), (f + 1, 0, f))[k]
        wide = ((f - 1, 1, f), (f + 1, 1, f), (f + 1, 0, f - 1), (f + 1, 1, f - 1))[k]
        targets = []
        for block, part, column in (near, wide):
            targets.append(((block % NF * 32 + part * 16 + w) * NF) + column % NF)
        first.append((source, targets[c]))
        second.append((source, targets[1 - c]))
    return first, second


def body(train_grads, test_feats):
    rows, width = train_grads.shape
    half = width // 2
    f, core = lax.axis_index("feat"), lax.axis_index("core")
    group = lax.axis_index(("ylo", "zhi"))
    place = jnp.stack([f, core]).astype(jnp.int32)
    up = [(i, (i + 1) % NF) for i in range(NF)]
    down = [(i, (i - 1) % NF) for i in range(NF)]

    left, right = train_grads[:, :half], train_grads[:, half:]
    before0 = lax.ppermute(left, "feat", up)
    after0 = lax.ppermute(left, "feat", down)
    before1 = lax.ppermute(right, "feat", up)
    after1 = lax.ppermute(right, "feat", down)

    tests = test_feats.shape[0] // NF
    lot = lax.axis_index(("zhi", "zlo"))
    eighth = lax.dynamic_index_in_dim(test_feats.reshape(NF, 8, tests // 8, width), lot, 1, keepdims=False)

    def asked_by(k):
        return lax.dynamic_index_in_dim(eighth, (f + k) % NF, 0, keepdims=False)

    asked = [asked_by(0)]
    for k in range(1, NF):
        asked.append(lax.ppermute(asked_by(-k), "feat", [(i, (i - k) % NF) for i in range(NF)]))
    queries = lax.all_gather(jnp.stack(asked), ("zhi", "zlo"), axis=1, tiled=True)

    far0 = lax.ppermute(before0, "feat", up)
    far1 = lax.ppermute(after1, "feat", down)

    near, got = chip_sum(*gram_units(near_kernel, place, (train_grads, before0, after0), NEAR_FLOPS))
    blocks = (train_grads, before0, before1, after0, after1)
    near = slice_sum(near)
    wide, _ = chip_sum(*gram_units(wide_kernel, place, blocks, WIDE_FLOPS, (got,)), near)
    scores = score_rows((train_grads, before0, before1, after0, after1, far0, far1), queries)
    wide = slice_sum(wide, scores)

    first_moves, second_moves = final_moves()
    first = lax.ppermute(jnp.where(core == 0, near, wide), AXES, first_moves)
    second = lax.ppermute(jnp.where(core == 0, wide, near), AXES, second_moves)
    apart = (group - f) % NF
    from_wide = (apart == 2) | ((apart % 2 == 1) & (lax.axis_index("zlo") >= 2))
    train_count = rows * 128
    gram = jnp.where(from_wide, jnp.concatenate([second, first]), jnp.concatenate([first, second]))
    gram = gram * (1.0 / F16_SCALE / train_count)

    return (scores, gram)


def solution(mesh):
    fine = Mesh(mesh.devices.reshape(2, 2, 4, 4, 2, 4), AXES)
    in_specs = (P(AXES[:5], "feat"), P(None, "feat"))
    out_specs = (P(AXES[:5], "feat"), P(AXES[:5], "feat"))
    return jax.shard_map(body, mesh=fine, in_specs=in_specs, out_specs=out_specs, check_vma=False)
```

```python
import jax
import jax.numpy as jnp
from jax import lax
from jax.experimental import pallas as pl
from jax.experimental.pallas import tpu as pltpu
from jax.sharding import Mesh, PartitionSpec as P

NF = 4
GRAM_FLOPS, GRAM_BYTES = 1 << 36, 1 << 30
SCORE_FLOPS, SCORE_BYTES = 1 << 36, 1 << 30
F16_SCALE = 2.0**-7
AXES = ("ylo", "zhi", "zlo", "x", "core", "feat")


def dot(a, b, on):
    return lax.dot_general(a, b, (((on,), (on,)), ((), ())), preferred_element_type=jnp.float32)


def gram_kernel(place, own, before0, before1, after0, after1, *rest):
    keep, send = rest[-2:]
    half = before0.shape[1]
    terms = (
        lambda: dot(own[...], own[...], 0),
        lambda: jnp.concatenate([dot(after0[...], own[...], 0), dot(after1[...], own[...], 0)]),
        lambda: jnp.concatenate(
            [
                jnp.concatenate([dot(a[...], b[...], 0) for b in (before0, before1)], axis=1)
                for a in (after0, after1)
            ]
        ),
        lambda: jnp.concatenate([dot(before0[...], own[...], 0), dot(before1[...], own[...], 0)]),
    )
    for k, term in enumerate(terms):

        @pl.when(pl.program_id(0) == k)
        def _():
            parts = term().reshape(16, 32, 2 * half)
            low, high = parts[:, :16], parts[:, 16:]
            first = place[1] == 0
            keep[0] = jnp.where(first, low, high)
            send[0] = jnp.where(first, high, low)


def gram_terms(place, blocks, earlier):
    rows, width = blocks[0].shape
    slot = pl.BlockSpec((1, 16, 16, width), lambda k, place: ((place[0] + k) % NF, 0, 0, 0))
    shape = jax.ShapeDtypeStruct((NF, 16, 16, width), jnp.float32)
    return pl.pallas_call(
        gram_kernel,
        out_shape=(shape, shape),
        grid_spec=pltpu.PrefetchScalarGridSpec(
            num_scalar_prefetch=1,
            grid=(NF,),
            in_specs=[pl.BlockSpec((rows, b.shape[1]), lambda k, place: (0, 0)) for b in blocks]
            + [pl.BlockSpec(memory_space=pl.ANY) for _ in earlier],
            out_specs=(slot, slot),
        ),
        compiler_params=pltpu.CompilerParams(vmem_limit_bytes=48 << 20),
        cost_estimate=pl.CostEstimate(flops=GRAM_FLOPS, bytes_accessed=GRAM_BYTES, transcendentals=0),
    )(place, *blocks, *earlier)


def scores_kernel(own, before0, before1, after0, after1, far0, far1, queries, scores):
    half = before0.shape[1]
    total = dot(own[:, :half], queries[0, 0], 1) + dot(own[:, half:], queries[0, 1], 1)
    for k, first, second in ((1, after0, after1), (2, far0, far1), (3, before0, before1)):
        total += dot(first[...], queries[k, 0], 1) + dot(second[...], queries[k, 1], 1)
    scores[...] = (total * (2 * half * NF) ** (-0.5)).astype(scores.dtype)


def score_rows(blocks, queries):
    rows, tests = blocks[0].shape[0], queries.shape[2]
    step = 256
    return pl.pallas_call(
        scores_kernel,
        out_shape=jax.ShapeDtypeStruct((rows, tests), jnp.bfloat16),
        grid=(rows // step,),
        in_specs=[pl.BlockSpec((step, b.shape[1]), lambda i: (i, 0)) for b in blocks]
        + [pl.BlockSpec(queries.shape, lambda i: (0, 0, 0, 0))],
        out_specs=pl.BlockSpec((step, tests), lambda i: (i, 0)),
        compiler_params=pltpu.CompilerParams(vmem_limit_bytes=40 << 20),
        cost_estimate=pl.CostEstimate(flops=SCORE_FLOPS, bytes_accessed=SCORE_BYTES, transcendentals=0),
    )(*blocks, queries)


def body(train_grads, test_feats):
    rows, width = train_grads.shape
    half = width // 2
    f, core = lax.axis_index("feat"), lax.axis_index("core")
    group = lax.axis_index(("ylo", "zhi"))
    place = jnp.stack([f, core]).astype(jnp.int32)
    up = [(i, (i + 1) % NF) for i in range(NF)]
    down = [(i, (i - 1) % NF) for i in range(NF)]

    lots = 32
    lot = lax.axis_index(("zhi", "zlo", "x"))
    tests = test_feats.shape[0] // NF
    mine = lax.dynamic_index_in_dim(test_feats.reshape(NF, lots, tests // lots, width), lot, 1, keepdims=False)

    def asked_by(k):
        piece = lax.dynamic_index_in_dim(mine, (f + k) % NF, 0, keepdims=False)
        return jnp.concatenate([piece[:, :half], piece[:, half:]])

    left, right = train_grads[:, :half], train_grads[:, half:]
    loads = (jnp.concatenate([left, asked_by(1)]), jnp.concatenate([right, asked_by(-1)]), asked_by(2))
    before0 = lax.ppermute(loads[0], "feat", up)
    after1 = lax.ppermute(loads[1], "feat", down)
    across = lax.ppermute(loads[2], "feat", [(i, (i + 2) % NF) for i in range(NF)])
    left, right, loads = lax.optimization_barrier((left, right, loads))
    before1 = lax.ppermute(right, "feat", up)
    after0 = lax.ppermute(left, "feat", down)

    pieces = jnp.stack([asked_by(0), after1[rows:], across, before0[rows:]]).reshape(NF, 2, tests // lots, half)
    shared = jnp.broadcast_to(pieces[None], (lots,) + pieces.shape)
    shared = lax.all_to_all(shared, ("zhi", "zlo", "x"), split_axis=0, concat_axis=0, tiled=True)
    queries = shared.transpose(1, 2, 0, 3, 4).reshape(NF, 2, tests, half)

    far0 = lax.ppermute(before0, "feat", up)
    far1 = lax.ppermute(after1, "feat", down)
    blocks = (train_grads, before0, before1, after0, after1)
    scores = score_rows(blocks + (far0, far1), queries)

    keep, send = gram_terms(place, blocks, ())
    got = lax.ppermute(send, "core", [(0, 1), (1, 0)])
    lots = ((keep + got) * F16_SCALE).astype(jnp.float16).reshape(64, 16, width)
    lots = lax.all_to_all(lots, AXES[:4], split_axis=0, concat_axis=0, tiled=True)
    lots, scores = lax.optimization_barrier((lots, scores))
    train_count = rows * 128
    summed = jnp.sum(lots.astype(jnp.float32), axis=0) * (1.0 / F16_SCALE / train_count)
    moves = [(((i + 2) % NF) * NF + i, ((i + 1) % NF) * NF + (i - 1) % NF) for i in range(NF)]
    moved = lax.ppermute(summed, ("ylo", "zhi", "feat"), moves)
    gram = jnp.where(group == (f + 2) % NF, moved, summed)
    return (scores, gram)


def solution(mesh):
    fine = Mesh(mesh.devices.reshape(2, 2, 4, 4, 2, 4), AXES)
    in_specs = (P(AXES[:5], "feat"), P(None, "feat"))
    out_specs = (P(AXES[:5], "feat"), P(AXES[:5], "feat"))
    return jax.shard_map(body, mesh=fine, in_specs=in_specs, out_specs=out_specs, check_vma=False)
```

```python
import jax
import jax.numpy as jnp
from jax import lax
from jax.experimental import pallas as pl
from jax.experimental.pallas import tpu as pltpu
from jax.sharding import Mesh, PartitionSpec as P

NF = 4
GRAM_FLOPS, GRAM_BYTES = 0, 0
SCORE_FLOPS, SCORE_BYTES = 1 << 36, 1 << 30
F16_SCALE = 2.0**-7
AXES = ("ylo", "zhi", "zlo", "x", "core", "feat")


def dot(a, b, on):
    return lax.dot_general(a, b, (((on,), (on,)), ((), ())), preferred_element_type=jnp.float32)


def gram_kernel(place, own, before0, before1, after0, after1, *rest):
    keep, send = rest[-2:]
    half = before0.shape[1]
    terms = (
        lambda: dot(own[...], own[...], 0),
        lambda: jnp.concatenate([dot(after0[...], own[...], 0), dot(after1[...], own[...], 0)]),
        lambda: jnp.concatenate(
            [
                jnp.concatenate([dot(a[...], b[...], 0) for b in (before0, before1)], axis=1)
                for a in (after0, after1)
            ]
        ),
        lambda: jnp.concatenate([dot(before0[...], own[...], 0), dot(before1[...], own[...], 0)]),
    )
    for k, term in enumerate(terms):

        @pl.when(pl.program_id(0) == k)
        def _():
            parts = term().reshape(16, 32, 2 * half)
            low, high = parts[:, :16], parts[:, 16:]
            first = place[1] == 0
            keep[0] = jnp.where(first, low, high)
            send[0] = jnp.where(first, high, low)


def gram_terms(place, blocks, earlier):
    rows, width = blocks[0].shape
    slot = pl.BlockSpec((1, 16, 16, width), lambda k, place: ((place[0] + k) % NF, 0, 0, 0))
    shape = jax.ShapeDtypeStruct((NF, 16, 16, width), jnp.float32)
    return pl.pallas_call(
        gram_kernel,
        out_shape=(shape, shape),
        grid_spec=pltpu.PrefetchScalarGridSpec(
            num_scalar_prefetch=1,
            grid=(NF,),
            in_specs=[pl.BlockSpec((rows, b.shape[1]), lambda k, place: (0, 0)) for b in blocks]
            + [pl.BlockSpec(memory_space=pl.ANY) for _ in earlier],
            out_specs=(slot, slot),
        ),
        compiler_params=pltpu.CompilerParams(vmem_limit_bytes=60 << 20),
        cost_estimate=pl.CostEstimate(flops=GRAM_FLOPS, bytes_accessed=GRAM_BYTES, transcendentals=0),
    )(place, *blocks, *earlier)


def scores_kernel(own, before0, before1, after0, after1, far0, far1, queries, scores):
    half = before0.shape[1]
    pairs = ((own[:, :half], own[:, half:]), (after0[...], after1[...]), (far0[...], far1[...]), (before0[...], before1[...]))
    total = jnp.zeros(scores.shape, jnp.float32)
    for k, pair in enumerate(pairs):
        for h, block in enumerate(pair):
            total += dot(block, queries[:, k, h].reshape(scores.shape[1], half), 1)
    scores[...] = (total * (2 * half * NF) ** (-0.5)).astype(scores.dtype)


def score_rows(blocks, queries):
    rows, tests = blocks[0].shape[0], queries.shape[0] * queries.shape[3]
    step = 256
    return pl.pallas_call(
        scores_kernel,
        out_shape=jax.ShapeDtypeStruct((rows, tests), jnp.bfloat16),
        grid=(rows // step,),
        in_specs=[pl.BlockSpec((step, b.shape[1]), lambda i: (i, 0)) for b in blocks]
        + [pl.BlockSpec(queries.shape, lambda i: (0,) * 5)],
        out_specs=pl.BlockSpec((step, tests), lambda i: (i, 0)),
        compiler_params=pltpu.CompilerParams(vmem_limit_bytes=60 << 20),
        cost_estimate=pl.CostEstimate(flops=SCORE_FLOPS, bytes_accessed=SCORE_BYTES, transcendentals=0),
    )(*blocks, queries)


def body(train_grads, test_feats):
    rows, width = train_grads.shape
    half = width // 2
    f, core = lax.axis_index("feat"), lax.axis_index("core")
    group = lax.axis_index(("ylo", "zhi"))
    place = jnp.stack([f, core]).astype(jnp.int32)
    up = [(i, (i + 1) % NF) for i in range(NF)]
    down = [(i, (i - 1) % NF) for i in range(NF)]

    lots = 4
    lot = lax.axis_index("x")
    tests = test_feats.shape[0] // NF
    mine = lax.dynamic_index_in_dim(test_feats.reshape(NF, lots, tests // lots, width), lot, 1, keepdims=False)

    def asked_by(k):
        piece = lax.dynamic_index_in_dim(mine, (f + k) % NF, 0, keepdims=False)
        return jnp.concatenate([piece[:, :half], piece[:, half:]])

    left, right = train_grads[:, :half], train_grads[:, half:]
    loads = (jnp.concatenate([left, asked_by(1)]), jnp.concatenate([right, asked_by(-1)]), asked_by(2))
    before0 = lax.ppermute(loads[0], "feat", up)
    after1 = lax.ppermute(loads[1], "feat", down)
    across = lax.ppermute(loads[2], "feat", [(i, (i + 2) % NF) for i in range(NF)])
    left, right, loads = lax.optimization_barrier((left, right, loads))
    before1 = lax.ppermute(right, "feat", up)
    after0 = lax.ppermute(left, "feat", down)

    pieces = jnp.stack([asked_by(0), after1[rows:], across, before0[rows:]]).reshape(NF, 2, tests // lots, half)
    queries = lax.all_gather(pieces, "x", axis=0, tiled=False)

    far0 = lax.ppermute(before0, "feat", up)
    far1 = lax.ppermute(after1, "feat", down)
    blocks = (train_grads, before0, before1, after0, after1)
    scores = score_rows(blocks + (far0, far1), queries)

    keep, send = gram_terms(place, blocks, (pieces,))
    got = lax.ppermute(send, "core", [(0, 1), (1, 0)])
    lots = ((keep + got) * F16_SCALE).astype(jnp.float16).reshape(64, 16, width)
    lots = lax.all_to_all(lots, AXES[:4], split_axis=0, concat_axis=0, tiled=True)
    lots, scores = lax.optimization_barrier((lots, scores))
    train_count = rows * 128
    summed = jnp.sum(lots.astype(jnp.float32), axis=0) * (1.0 / F16_SCALE / train_count)
    moves = [(((i + 2) % NF) * NF + i, ((i + 1) % NF) * NF + (i - 1) % NF) for i in range(NF)]
    moved = lax.ppermute(summed, ("ylo", "zhi", "feat"), moves)
    gram = jnp.where(group == (f + 2) % NF, moved, summed)
    return (scores, gram)


def solution(mesh):
    fine = Mesh(mesh.devices.reshape(2, 2, 4, 4, 2, 4), AXES)
    in_specs = (P(AXES[:5], "feat"), P(None, "feat"))
    out_specs = (P(AXES[:5], "feat"), P(AXES[:5], "feat"))
    return jax.shard_map(body, mesh=fine, in_specs=in_specs, out_specs=out_specs, check_vma=False)
```

```python
import jax
import jax.numpy as jnp
from jax import lax
from jax.experimental import pallas as pl
from jax.experimental.pallas import tpu as pltpu
from jax.sharding import Mesh, PartitionSpec as P

NF = 4
GRAM_FLOPS, GRAM_BYTES = 1<<36, 1<<30
SCORE_FLOPS, SCORE_BYTES = 1 << 36, 1 << 30
F16_SCALE = 2.0**-7
AXES = ("ylo", "zhi", "zlo", "x", "core", "feat")


def dot(a, b, on):
    return lax.dot_general(a, b, (((on,), (on,)), ((), ())), preferred_element_type=jnp.float32)


def store_unit(place, product, keep, send):
    parts = product.reshape(8, 32, product.shape[1])
    low, high = parts[:, :16], parts[:, 16:]
    first = place[1] == 0
    keep[0] = jnp.where(first, low, high)
    send[0] = jnp.where(first, high, low)


def each_step(steps, place, keep, send):
    for k, step in enumerate(steps):

        @pl.when(pl.program_id(0) == k)
        def _():
            store_unit(place, step(), keep, send)


def first_kernel(place, own, before0, after1, keep, send):
    half = before0.shape[1]
    steps = (
        lambda: dot(own[:, :half], own[...], 0),
        lambda: dot(own[:, half:], own[...], 0),
        lambda: dot(before0[...], own[...], 0),
        lambda: dot(after1[...], own[...], 0),
    )
    each_step(steps, place, keep, send)


def second_kernel(place, own, before0, before1, after0, after1, *rest):
    keep, send = rest[-2:]

    def across(after):
        return jnp.concatenate([dot(after[...], b[...], 0) for b in (before0, before1)], axis=1)

    steps = (
        lambda: dot(before1[...], own[...], 0),
        lambda: dot(after0[...], own[...], 0),
        lambda: across(after0),
        lambda: across(after1),
    )
    each_step(steps, place, keep, send)


def gram_terms(kernel, slots, halves, place, blocks, kept=(), earlier=()):
    rows, width = blocks[0].shape

    def at(k, place):
        slot = sum(jnp.where(k == i, s, 0) for i, s in enumerate(slots))
        part = sum(jnp.where(k == i, h, 0) for i, h in enumerate(halves))
        return ((place[0] + slot) % NF, part, 0, 0)

    unit = pl.BlockSpec((1, 8, 16, width), at)
    shape = jax.ShapeDtypeStruct((NF, 16, 16, width), jnp.float32)
    taken = 1 + len(blocks)
    return pl.pallas_call(
        kernel,
        out_shape=(shape, shape),
        grid_spec=pltpu.PrefetchScalarGridSpec(
            num_scalar_prefetch=1,
            grid=(len(slots),),
            in_specs=[pl.BlockSpec((rows, b.shape[1]), lambda k, place: (0, 0)) for b in blocks]
            + [pl.BlockSpec(memory_space=pl.ANY) for _ in (*kept, *earlier)],
            out_specs=(unit, unit),
        ),
        input_output_aliases={taken + i: i for i in range(len(kept))},
        compiler_params=pltpu.CompilerParams(vmem_limit_bytes=60 << 20),
        cost_estimate=pl.CostEstimate(flops=GRAM_FLOPS, bytes_accessed=GRAM_BYTES, transcendentals=0),
    )(place, *blocks, *kept, *earlier)


def scores_kernel(own, before0, before1, after0, after1, far0, far1, queries, scores):
    half = before0.shape[1]
    pairs = ((own[:, :half], own[:, half:]), (after0[...], after1[...]), (far0[...], far1[...]), (before0[...], before1[...]))
    total = jnp.zeros(scores.shape, jnp.float32)
    for k, pair in enumerate(pairs):
        for h, block in enumerate(pair):
            total += dot(block, queries[:, k, h].reshape(scores.shape[1], half), 1)
    scores[...] = (total * (2 * half * NF) ** (-0.5)).astype(scores.dtype)


def score_rows(blocks, queries):
    rows, tests = blocks[0].shape[0], queries.shape[0] * queries.shape[3]
    step = 256
    return pl.pallas_call(
        scores_kernel,
        out_shape=jax.ShapeDtypeStruct((rows, tests), jnp.bfloat16),
        grid=(rows // step,),
        in_specs=[pl.BlockSpec((step, b.shape[1]), lambda i: (i, 0)) for b in blocks]
        + [pl.BlockSpec(queries.shape, lambda i: (0,) * 5)],
        out_specs=pl.BlockSpec((step, tests), lambda i: (i, 0)),
        compiler_params=pltpu.CompilerParams(vmem_limit_bytes=60 << 20),
        cost_estimate=pl.CostEstimate(flops=SCORE_FLOPS, bytes_accessed=SCORE_BYTES, transcendentals=0),
    )(*blocks, queries)


def body(train_grads, test_feats):
    rows, width = train_grads.shape
    half = width // 2
    f, core = lax.axis_index("feat"), lax.axis_index("core")
    group = lax.axis_index(("ylo", "zhi"))
    place = jnp.stack([f, core]).astype(jnp.int32)
    up = [(i, (i + 1) % NF) for i in range(NF)]
    down = [(i, (i - 1) % NF) for i in range(NF)]

    lots = 8
    lot = lax.axis_index(("x", "core"))
    tests = test_feats.shape[0] // NF
    mine = lax.dynamic_index_in_dim(test_feats.reshape(NF, lots, tests // lots, width), lot, 1, keepdims=False)

    def asked_by(k):
        piece = lax.dynamic_index_in_dim(mine, (f + k) % NF, 0, keepdims=False)
        return jnp.concatenate([piece[:, :half], piece[:, half:]])

    left, right = train_grads[:, :half], train_grads[:, half:]
    loads = (jnp.concatenate([left, asked_by(1)]), jnp.concatenate([right, asked_by(-1)]), asked_by(2))
    before0 = lax.ppermute(loads[0], "feat", up)
    after1 = lax.ppermute(loads[1], "feat", down)
    across = lax.ppermute(loads[2], "feat", [(i, (i + 2) % NF) for i in range(NF)])
    left, right, loads = lax.optimization_barrier((left, right, loads))
    before1 = lax.ppermute(right, "feat", up)
    after0 = lax.ppermute(left, "feat", down)

    pieces = jnp.stack([asked_by(0), after1[rows:], across, before0[rows:]]).reshape(NF, 2, tests // lots, half)
    shared = jnp.broadcast_to(pieces[None], (lots,) + pieces.shape)
    queries = lax.all_to_all(shared, ("x", "core"), split_axis=0, concat_axis=0, tiled=True)

    far0 = lax.ppermute(before0, "feat", up)
    far1 = lax.ppermute(after1, "feat", down)
    blocks = (train_grads, before0, before1, after0, after1)
    scores = score_rows(blocks + (far0, far1), queries)

    kept = gram_terms(first_kernel, (0, 0, 3, 1), (0, 1, 0, 1), place, (train_grads, before0, after1), earlier=())
    keep, send = gram_terms(second_kernel, (3, 1, 2, 2), (1, 0, 0, 1), place, blocks, kept, (queries,))
    got = lax.ppermute(send, "core", [(0, 1), (1, 0)])
    lots = ((keep + got) * F16_SCALE).astype(jnp.float16).reshape(64, 16, width)
    lots = lax.all_to_all(lots, AXES[:4], split_axis=0, concat_axis=0, tiled=True)
    lots, scores = lax.optimization_barrier((lots, scores))
    train_count = rows * 128
    summed = jnp.sum(lots.astype(jnp.float32), axis=0) * (1.0 / F16_SCALE / train_count)
    moves = [(((i + 2) % NF) * NF + i, ((i + 1) % NF) * NF + (i - 1) % NF) for i in range(NF)]
    moved = lax.ppermute(summed, ("ylo", "zhi", "feat"), moves)
    gram = jnp.where(group == (f + 2) % NF, moved, summed)
    return (scores, gram)


def solution(mesh):
    fine = Mesh(mesh.devices.reshape(2, 2, 4, 4, 2, 4), AXES)
    in_specs = (P(AXES[:5], "feat"), P(None, "feat"))
    out_specs = (P(AXES[:5], "feat"), P(AXES[:5], "feat"))
    return jax.shard_map(body, mesh=fine, in_specs=in_specs, out_specs=out_specs, check_vma=False)
```

```python
import jax
import jax.numpy as jnp
from jax import lax
from jax.experimental import pallas as pl
from jax.experimental.pallas import tpu as pltpu
from jax.sharding import Mesh, PartitionSpec as P

NF = 4
GRAM_FLOPS, GRAM_BYTES = 1<<36, 1<<30
SCORE_FLOPS, SCORE_BYTES = 1 << 36, 1 << 30
F16_SCALE = 2.0**-7
AXES = ("ylo", "zhi", "zlo", "x", "core", "feat")


def dot(a, b, on):
    return lax.dot_general(a, b, (((on,), (on,)), ((), ())), preferred_element_type=jnp.float32)


def store_unit(place, product, keep, send):
    parts = product.reshape(8, 32, product.shape[1])
    low, high = parts[:, :16], parts[:, 16:]
    first = place[1] == 0
    keep[0, :, 0] = jnp.where(first, low, high)
    send[0, :, 0] = jnp.where(first, high, low)


def each_step(steps, place, keep, send):
    for k, step in enumerate(steps):

        @pl.when(pl.program_id(0) == k)
        def _():
            store_unit(place, step(), keep, send)


def first_kernel(place, own, before0, after1, keep, send):
    half = before0.shape[1]
    steps = (
        lambda: dot(own[:, :half], own[...], 0),
        lambda: dot(own[:, half:], own[...], 0),
        lambda: dot(before0[...], own[...], 0),
        lambda: dot(after1[...], own[...], 0),
    )
    each_step(steps, place, keep, send)


def second_kernel(place, own, before0, before1, after0, after1, *rest):
    keep, send = rest[-2:]

    def across(after):
        return jnp.concatenate([dot(after[...], b[...], 0) for b in (before0, before1)], axis=1)

    steps = (
        lambda: dot(before1[...], own[...], 0),
        lambda: dot(after0[...], own[...], 0),
        lambda: across(after0),
        lambda: across(after1),
    )
    each_step(steps, place, keep, send)


def gram_terms(kernel, slots, halves, place, blocks, kept=(), earlier=()):
    rows, width = blocks[0].shape

    def at(k, place):
        slot = sum(jnp.where(k == i, s, 0) for i, s in enumerate(slots))
        part = sum(jnp.where(k == i, h, 0) for i, h in enumerate(halves))
        slot = (place[0] + slot) % NF
        return (slot % 2, part, slot // 2, 0, 0)

    unit = pl.BlockSpec((1, 8, 1, 16, width), at)
    shape = jax.ShapeDtypeStruct((2, 16, 2, 16, width), jnp.float32)
    taken = 1 + len(blocks)
    return pl.pallas_call(
        kernel,
        out_shape=(shape, shape),
        grid_spec=pltpu.PrefetchScalarGridSpec(
            num_scalar_prefetch=1,
            grid=(len(slots),),
            in_specs=[pl.BlockSpec((rows, b.shape[1]), lambda k, place: (0, 0)) for b in blocks]
            + [pl.BlockSpec(memory_space=pl.ANY) for _ in (*kept, *earlier)],
            out_specs=(unit, unit),
        ),
        input_output_aliases={taken + i: i for i in range(len(kept))},
        compiler_params=pltpu.CompilerParams(vmem_limit_bytes=60 << 20),
        cost_estimate=pl.CostEstimate(flops=GRAM_FLOPS, bytes_accessed=GRAM_BYTES, transcendentals=0),
    )(place, *blocks, *kept, *earlier)


def scores_kernel(own, before0, before1, after0, after1, far0, far1, queries, scores):
    half = before0.shape[1]
    pairs = ((own[:, :half], own[:, half:]), (after0[...], after1[...]), (far0[...], far1[...]), (before0[...], before1[...]))
    total = jnp.zeros(scores.shape, jnp.float32)
    for k, pair in enumerate(pairs):
        for h, block in enumerate(pair):
            total += dot(block, queries[:, k, h].reshape(scores.shape[1], half), 1)
    scores[...] = (total * (2 * half * NF) ** (-0.5)).astype(scores.dtype)


def score_rows(blocks, queries):
    rows, tests = blocks[0].shape[0], queries.shape[0] * queries.shape[3]
    step = 256
    return pl.pallas_call(
        scores_kernel,
        out_shape=jax.ShapeDtypeStruct((rows, tests), jnp.bfloat16),
        grid=(rows // step,),
        in_specs=[pl.BlockSpec((step, b.shape[1]), lambda i: (i, 0)) for b in blocks]
        + [pl.BlockSpec(queries.shape, lambda i: (0,) * 5)],
        out_specs=pl.BlockSpec((step, tests), lambda i: (i, 0)),
        compiler_params=pltpu.CompilerParams(vmem_limit_bytes=60 << 20),
        cost_estimate=pl.CostEstimate(flops=SCORE_FLOPS, bytes_accessed=SCORE_BYTES, transcendentals=0),
    )(*blocks, queries)


def final_moves():
    def owner(slot, f):
        return (slot - 1) % NF * NF + (f - 1) % NF if slot == (f + 2) % NF else slot * NF + f

    places = [(g, f) for g in range(NF) for f in range(NF)]
    across = [(g * NF + f, owner(g, f)) for g, f in places if g == (f + 2) % NF]
    paired = [(g * NF + f, owner((g + 2) % NF, f)) for g, f in places]
    return across, paired


def body(train_grads, test_feats):
    rows, width = train_grads.shape
    half = width // 2
    f, core = lax.axis_index("feat"), lax.axis_index("core")
    group = lax.axis_index(("ylo", "zhi"))
    place = jnp.stack([f, core]).astype(jnp.int32)
    up = [(i, (i + 1) % NF) for i in range(NF)]
    down = [(i, (i - 1) % NF) for i in range(NF)]

    lots = 8
    lot = lax.axis_index(("x", "core"))
    tests = test_feats.shape[0] // NF
    mine = lax.dynamic_index_in_dim(test_feats.reshape(NF, lots, tests // lots, width), lot, 1, keepdims=False)

    def asked_by(k):
        piece = lax.dynamic_index_in_dim(mine, (f + k) % NF, 0, keepdims=False)
        return jnp.concatenate([piece[:, :half], piece[:, half:]])

    left, right = train_grads[:, :half], train_grads[:, half:]
    loads = (jnp.concatenate([left, asked_by(1)]), jnp.concatenate([right, asked_by(-1)]), asked_by(2))
    before0 = lax.ppermute(loads[0], "feat", up)
    after1 = lax.ppermute(loads[1], "feat", down)
    across = lax.ppermute(loads[2], "feat", [(i, (i + 2) % NF) for i in range(NF)])
    left, right, loads = lax.optimization_barrier((left, right, loads))
    before1 = lax.ppermute(right, "feat", up)
    after0 = lax.ppermute(left, "feat", down)

    pieces = jnp.stack([asked_by(0), after1[rows:], across, before0[rows:]]).reshape(NF, 2, tests // lots, half)
    shared = jnp.broadcast_to(pieces[None], (lots,) + pieces.shape)
    queries = lax.all_to_all(shared, ("x", "core"), split_axis=0, concat_axis=0, tiled=True)

    far0 = lax.ppermute(before0, "feat", up)
    far1 = lax.ppermute(after1, "feat", down)
    blocks = (train_grads, before0, before1, after0, after1)
    scores = score_rows(blocks + (far0, far1), queries)

    kept = gram_terms(first_kernel, (0, 0, 3, 1), (0, 1, 0, 1), place, (train_grads, before0, after1), earlier=())
    keep, send = gram_terms(second_kernel, (3, 1, 2, 2), (1, 0, 0, 1), place, blocks, kept, (queries,))
    got = lax.ppermute(send, "core", [(0, 1), (1, 0)])
    lots = ((keep + got) * F16_SCALE).astype(jnp.float16).reshape(32, 2, 16, width)
    lots = lax.all_to_all(lots, AXES[1:4], split_axis=0, concat_axis=0, tiled=True)
    lots, scores = lax.optimization_barrier((lots, scores))
    train_count = rows * 128
    summed = jnp.sum(lots.astype(jnp.float32), axis=0) * (1.0 / F16_SCALE / train_count)

    ylo = lax.axis_index("ylo")
    mine = lax.dynamic_index_in_dim(summed, ylo, 0, keepdims=False)
    other = lax.dynamic_index_in_dim(summed, 1 - ylo, 0, keepdims=False)
    across, paired = final_moves()
    moved = lax.ppermute(mine, ("ylo", "zhi", "feat"), across)
    added = lax.ppermute(other, ("ylo", "zhi", "feat"), paired)
    gram = jnp.where(group == (f + 2) % NF, moved, mine) + added
    return (scores, gram)


def solution(mesh):
    fine = Mesh(mesh.devices.reshape(2, 2, 4, 4, 2, 4), AXES)
    in_specs = (P(AXES[:5], "feat"), P(None, "feat"))
    out_specs = (P(AXES[:5], "feat"), P(AXES[:5], "feat"))
    return jax.shard_map(body, mesh=fine, in_specs=in_specs, out_specs=out_specs, check_vma=False)
```

```python
import jax
import jax.numpy as jnp
from jax import lax
from jax.experimental import pallas as pl
from jax.experimental.pallas import tpu as pltpu
from jax.sharding import Mesh, PartitionSpec as P

NF = 4
GRAM_FLOPS, GRAM_BYTES = 0, 0
SCORE_FLOPS, SCORE_BYTES = 1 << 36, 1 << 30
F16_SCALE = 2.0**-7
AXES = ("ylo", "zhi", "zlo", "x", "core", "feat")


def dot(a, b, on):
    return lax.dot_general(a, b, (((on,), (on,)), ((), ())), preferred_element_type=jnp.float32)


def first_kernel(place, *refs):
    out = refs[-1]
    half = out.shape[-1] // 2
    even = place[1] == 0

    def product(step):
        total = None
        for own, before0, after1 in (refs[:3], refs[3:6]):
            first, second = ((own[:, :half], own[:, half:]), (before0[...], after1[...]))[step]
            term = dot(jnp.where(even, first, second), own[...], 0)
            total = term if total is None else total + term
        return total

    for step in range(2):

        @pl.when(pl.program_id(0) == step)
        def _():
            out[0] = product(step).reshape(out.shape[1:])


def second_kernel(place, *refs):
    out = refs[-1]
    even = place[1] == 0

    def product(step):
        total = None
        for own, before0, before1, after0, after1 in (refs[:5], refs[5:10]):
            if step == 0:
                term = dot(jnp.where(even, after0[...], before1[...]), own[...], 0)
            else:
                left = jnp.where(even, after0[...], after1[...])
                term = jnp.concatenate([dot(left, before0[...], 0), dot(left, before1[...], 0)], axis=1)
            total = term if total is None else total + term
        return total

    for step in range(2):

        @pl.when(pl.program_id(0) == step)
        def _():
            out[0] = product(step).reshape(out.shape[1:])


def gram_terms(kernel, slots, place, blocks, kept=(), earlier=()):
    rows, width = blocks[0].shape

    def at(k, place):
        even, odd = (jnp.where(k == 0, pair[0], pair[1]) for pair in slots)
        return ((place[0] + jnp.where(place[1] == 0, even, odd)) % NF, 0, 0, 0)

    return pl.pallas_call(
        kernel,
        out_shape=jax.ShapeDtypeStruct((NF, 16, 16, width), jnp.float32),
        grid_spec=pltpu.PrefetchScalarGridSpec(
            num_scalar_prefetch=1,
            grid=(2,),
            in_specs=[pl.BlockSpec((rows, b.shape[1]), lambda k, place: (0, 0)) for b in blocks]
            + [pl.BlockSpec(memory_space=pl.ANY) for _ in (*kept, *earlier)],
            out_specs=pl.BlockSpec((1, 16, 16, width), at),
        ),
        input_output_aliases={1 + len(blocks): 0} if kept else {},
        compiler_params=pltpu.CompilerParams(vmem_limit_bytes=60 << 20),
        cost_estimate=pl.CostEstimate(flops=GRAM_FLOPS, bytes_accessed=GRAM_BYTES, transcendentals=0),
    )(place, *blocks, *kept, *earlier)


def final_moves():
    moves = []
    for source in range(512):
        f, c, w, g = source % 4, source // 4 % 2, source // 8 % 16, source // 128
        lot = c * 16 + w
        if g == (f + 2) % NF:
            g, f = (g - 1) % NF, (f - 1) % NF
        moves.append((source, (g * 32 + lot) * NF + f))
    return moves


def scores_kernel(own, before0, before1, after0, after1, far0, far1, queries, scores):
    half = before0.shape[1]
    pairs = ((own[:, :half], own[:, half:]), (after0[...], after1[...]), (far0[...], far1[...]), (before0[...], before1[...]))
    total = jnp.zeros(scores.shape, jnp.float32)
    for k, pair in enumerate(pairs):
        for h, block in enumerate(pair):
            total += dot(block, queries[:, k, h].reshape(scores.shape[1], half), 1)
    scores[...] = (total * (2 * half * NF) ** (-0.5)).astype(scores.dtype)


def score_rows(blocks, queries):
    rows, tests = blocks[0].shape[0], queries.shape[0] * queries.shape[3]
    step = 256
    return pl.pallas_call(
        scores_kernel,
        out_shape=jax.ShapeDtypeStruct((rows, tests), jnp.bfloat16),
        grid=(rows // step,),
        in_specs=[pl.BlockSpec((step, b.shape[1]), lambda i: (i, 0)) for b in blocks]
        + [pl.BlockSpec(queries.shape, lambda i: (0,) * 5)],
        out_specs=pl.BlockSpec((step, tests), lambda i: (i, 0)),
        compiler_params=pltpu.CompilerParams(vmem_limit_bytes=60 << 20),
        cost_estimate=pl.CostEstimate(flops=SCORE_FLOPS, bytes_accessed=SCORE_BYTES, transcendentals=0),
    )(*blocks, queries)


def body(train_grads, test_feats):
    rows, width = train_grads.shape
    half = width // 2
    f, core = lax.axis_index("feat"), lax.axis_index("core")
    place = jnp.stack([f, core]).astype(jnp.int32)
    up = [(i, (i + 1) % NF) for i in range(NF)]
    down = [(i, (i - 1) % NF) for i in range(NF)]

    lots = 8
    lot = lax.axis_index(("x", "core"))
    tests = test_feats.shape[0] // NF
    mine = lax.dynamic_index_in_dim(test_feats.reshape(NF, lots, tests // lots, width), lot, 1, keepdims=False)

    def asked_by(k):
        piece = lax.dynamic_index_in_dim(mine, (f + k) % NF, 0, keepdims=False)
        return jnp.concatenate([piece[:, :half], piece[:, half:]])

    left, right = train_grads[:, :half], train_grads[:, half:]
    loads = (jnp.concatenate([left, asked_by(1)]), jnp.concatenate([right, asked_by(-1)]), asked_by(2))
    before0 = lax.ppermute(loads[0], "feat", up)
    after1 = lax.ppermute(loads[1], "feat", down)
    across = lax.ppermute(loads[2], "feat", [(i, (i + 2) % NF) for i in range(NF)])
    left, right, loads = lax.optimization_barrier((left, right, loads))
    before1 = lax.ppermute(right, "feat", up)
    after0 = lax.ppermute(left, "feat", down)

    pieces = jnp.stack([asked_by(0), after1[rows:], across, before0[rows:]]).reshape(NF, 2, tests // lots, half)
    shared = jnp.broadcast_to(pieces[None], (lots,) + pieces.shape)
    queries = lax.all_to_all(shared, ("x", "core"), split_axis=0, concat_axis=0, tiled=True)

    far0 = lax.ppermute(before0, "feat", up)
    far1 = lax.ppermute(after1, "feat", down)
    blocks = (train_grads, before0, before1, after0, after1)
    scores = score_rows(blocks + (far0, far1), queries)

    def swap(block):
        return lax.ppermute(block, "core", [(0, 1), (1, 0)])

    swapped = [swap(block) for block in blocks]
    early = [theirs for group in (blocks, swapped) for theirs in (group[0], group[1], group[4])]
    kept = gram_terms(first_kernel, ((0, 3), (0, 1)), place, early)
    terms = gram_terms(second_kernel, ((1, 2), (3, 2)), place, (*blocks, *swapped), (kept,), (queries,))
    sums = (terms * F16_SCALE).astype(jnp.float16).reshape(64, 16, width)
    sums = lax.all_to_all(sums, AXES[:4], split_axis=0, concat_axis=0, tiled=True)
    sums, scores = lax.optimization_barrier((sums, scores))
    train_count = rows * 128
    summed = jnp.sum(sums.astype(jnp.float32), axis=0) * (1.0 / F16_SCALE / train_count)
    gram = lax.ppermute(summed, AXES, final_moves())
    return (scores, gram)


def solution(mesh):
    fine = Mesh(mesh.devices.reshape(2, 2, 4, 4, 2, 4), AXES)
    in_specs = (P(AXES[:5], "feat"), P(None, "feat"))
    out_specs = (P(AXES[:5], "feat"), P(AXES[:5], "feat"))
    return jax.shard_map(body, mesh=fine, in_specs=in_specs, out_specs=out_specs, check_vma=False)
```

```python
import jax
import jax.numpy as jnp
from jax import lax
from jax.experimental import pallas as pl
from jax.experimental.pallas import tpu as pltpu
from jax.sharding import Mesh, PartitionSpec as P

NF = 4
GRAM_FLOPS, GRAM_BYTES = 1<<36, 1<<30
SCORE_FLOPS, SCORE_BYTES = 1 << 36, 1 << 30
F16_SCALE = 2.0**-7
AXES = ("ylo", "zhi", "zlo", "x", "core", "feat")


def dot(a, b, on):
    return lax.dot_general(a, b, (((on,), (on,)), ((), ())), preferred_element_type=jnp.float32)


def store_unit(place, product, keep, send):
    parts = product.reshape(8, 32, product.shape[1])
    low, high = parts[:, :16], parts[:, 16:]
    first = place[1] == 0
    keep[0] = jnp.where(first, low, high)
    send[0] = jnp.where(first, high, low)


def each_step(steps, place, keep, send):
    for k, step in enumerate(steps):

        @pl.when(pl.program_id(0) == k)
        def _():
            store_unit(place, step(), keep, send)


def first_kernel(place, own, before0, after1, keep, send):
    half = before0.shape[1]
    steps = (
        lambda: dot(own[:, :half], own[...], 0),
        lambda: dot(own[:, half:], own[...], 0),
        lambda: dot(before0[...], own[...], 0),
        lambda: dot(after1[...], own[...], 0),
    )
    each_step(steps, place, keep, send)


def second_kernel(place, own, before0, before1, after0, after1, *rest):
    keep, send = rest[-2:]

    def across(after):
        return jnp.concatenate([dot(after[...], b[...], 0) for b in (before0, before1)], axis=1)

    steps = (
        lambda: dot(before1[...], own[...], 0),
        lambda: dot(after0[...], own[...], 0),
        lambda: across(after0),
        lambda: across(after1),
    )
    each_step(steps, place, keep, send)


def gram_terms(kernel, slots, halves, place, blocks, kept=(), earlier=()):
    rows, width = blocks[0].shape

    def at(k, place):
        slot = sum(jnp.where(k == i, s, 0) for i, s in enumerate(slots))
        part = sum(jnp.where(k == i, h, 0) for i, h in enumerate(halves))
        return ((place[0] + slot) % NF, part, 0, 0)

    unit = pl.BlockSpec((1, 8, 16, width), at)
    shape = jax.ShapeDtypeStruct((NF, 16, 16, width), jnp.float32)
    taken = 1 + len(blocks)
    return pl.pallas_call(
        kernel,
        out_shape=(shape, shape),
        grid_spec=pltpu.PrefetchScalarGridSpec(
            num_scalar_prefetch=1,
            grid=(len(slots),),
            in_specs=[pl.BlockSpec((rows, b.shape[1]), lambda k, place: (0, 0)) for b in blocks]
            + [pl.BlockSpec(memory_space=pl.ANY) for _ in (*kept, *earlier)],
            out_specs=(unit, unit),
        ),
        input_output_aliases={taken + i: i for i in range(len(kept))},
        compiler_params=pltpu.CompilerParams(vmem_limit_bytes=60 << 20),
        cost_estimate=pl.CostEstimate(flops=GRAM_FLOPS, bytes_accessed=GRAM_BYTES, transcendentals=0),
    )(place, *blocks, *kept, *earlier)


def scores_kernel(place, own, before0, before1, after0, after1, far0, far1, shared, swapped, scores):
    half = before0.shape[1]
    pairs = ((own[:, :half], own[:, half:]), (after0[...], after1[...]), (far0[...], far1[...]), (before0[...], before1[...]))
    total = jnp.zeros(scores.shape, jnp.float32)
    first = place[1] == 0
    for k, pair in enumerate(pairs):
        for h, block in enumerate(pair):
            mine, theirs = shared[:, k, h], swapped[:, k, h]
            asked = jnp.stack([jnp.where(first, mine, theirs), jnp.where(first, theirs, mine)], axis=1)
            total += dot(block, asked.reshape(scores.shape[1], half), 1)
    scores[...] = (total * (2 * half * NF) ** (-0.5)).astype(scores.dtype)


def score_rows(place, blocks, shared, swapped):
    rows, tests = blocks[0].shape[0], 2 * shared.shape[0] * shared.shape[3]
    step = 256
    return pl.pallas_call(
        scores_kernel,
        out_shape=jax.ShapeDtypeStruct((rows, tests), jnp.bfloat16),
        grid_spec=pltpu.PrefetchScalarGridSpec(
            num_scalar_prefetch=1,
            grid=(rows // step,),
            in_specs=[pl.BlockSpec((step, b.shape[1]), lambda i, place: (i, 0)) for b in blocks]
            + [pl.BlockSpec(shared.shape, lambda i, place: (0,) * 5) for _ in range(2)],
            out_specs=pl.BlockSpec((step, tests), lambda i, place: (i, 0)),
        ),
        compiler_params=pltpu.CompilerParams(vmem_limit_bytes=60 << 20),
        cost_estimate=pl.CostEstimate(flops=SCORE_FLOPS, bytes_accessed=SCORE_BYTES, transcendentals=0),
    )(place, *blocks, shared, swapped)


def body(train_grads, test_feats):
    rows, width = train_grads.shape
    half = width // 2
    f, core = lax.axis_index("feat"), lax.axis_index("core")
    group = lax.axis_index(("ylo", "zhi"))
    place = jnp.stack([f, core]).astype(jnp.int32)
    up = [(i, (i + 1) % NF) for i in range(NF)]
    down = [(i, (i - 1) % NF) for i in range(NF)]

    lots = 8
    lot = lax.axis_index(("x", "core"))
    tests = test_feats.shape[0] // NF
    mine = lax.dynamic_index_in_dim(test_feats.reshape(NF, lots, tests // lots, width), lot, 1, keepdims=False)

    def asked_by(k):
        piece = lax.dynamic_index_in_dim(mine, (f + k) % NF, 0, keepdims=False)
        return jnp.concatenate([piece[:, :half], piece[:, half:]])

    left, right = train_grads[:, :half], train_grads[:, half:]
    loads = (jnp.concatenate([left, asked_by(1)]), jnp.concatenate([right, asked_by(-1)]), asked_by(2))
    before0 = lax.ppermute(loads[0], "feat", up)
    after1 = lax.ppermute(loads[1], "feat", down)
    across = lax.ppermute(loads[2], "feat", [(i, (i + 2) % NF) for i in range(NF)])
    left, right, loads = lax.optimization_barrier((left, right, loads))
    before1 = lax.ppermute(right, "feat", up)
    after0 = lax.ppermute(left, "feat", down)

    pieces = jnp.stack([asked_by(0), after1[rows:], across, before0[rows:]]).reshape(NF, 2, tests // lots, half)
    shared = jnp.broadcast_to(pieces[None], (lots // 2,) + pieces.shape)
    shared = lax.all_to_all(shared, "x", split_axis=0, concat_axis=0, tiled=True)
    swapped = lax.ppermute(shared, "core", [(0, 1), (1, 0)])

    far0 = lax.ppermute(before0, "feat", up)
    far1 = lax.ppermute(after1, "feat", down)
    blocks = (train_grads, before0, before1, after0, after1)
    scores = score_rows(place, blocks + (far0, far1), shared, swapped)

    kept = gram_terms(first_kernel, (0, 0, 3, 1), (0, 1, 0, 1), place, (train_grads, before0, after1), earlier=())
    keep, send = gram_terms(second_kernel, (3, 1, 2, 2), (1, 0, 0, 1), place, blocks, kept, (shared,))
    got = lax.ppermute(send, "core", [(0, 1), (1, 0)])
    lots = ((keep + got) * F16_SCALE).astype(jnp.float16).reshape(64, 16, width)
    lots = lax.all_to_all(lots, AXES[:4], split_axis=0, concat_axis=0, tiled=True)
    lots, scores = lax.optimization_barrier((lots, scores))
    train_count = rows * 128
    summed = jnp.sum(lots.astype(jnp.float32), axis=0) * (1.0 / F16_SCALE / train_count)
    moves = [(((i + 2) % NF) * NF + i, ((i + 1) % NF) * NF + (i - 1) % NF) for i in range(NF)]
    moved = lax.ppermute(summed, ("ylo", "zhi", "feat"), moves)
    gram = jnp.where(group == (f + 2) % NF, moved, summed)
    return (scores, gram)


def solution(mesh):
    fine = Mesh(mesh.devices.reshape(2, 2, 4, 4, 2, 4), AXES)
    in_specs = (P(AXES[:5], "feat"), P(None, "feat"))
    out_specs = (P(AXES[:5], "feat"), P(AXES[:5], "feat"))
    return jax.shard_map(body, mesh=fine, in_specs=in_specs, out_specs=out_specs, check_vma=False)
```

```python
import jax
import jax.numpy as jnp
from jax import lax
from jax.experimental import pallas as pl
from jax.experimental.pallas import tpu as pltpu
from jax.sharding import Mesh, PartitionSpec as P

NF = 4
GRAM_FLOPS, GRAM_BYTES = 1<<36, 1<<30
SCORE_FLOPS, SCORE_BYTES = 1 << 30, 6 << 20
F16_SCALE = 2.0**-7
AXES = ("ylo", "zhi", "zlo", "x", "core", "feat")


def dot(a, b, on):
    return lax.dot_general(a, b, (((on,), (on,)), ((), ())), preferred_element_type=jnp.float32)


def store_unit(place, product, keep, send):
    parts = product.reshape(8, 32, product.shape[1])
    low, high = parts[:, :16], parts[:, 16:]
    first = place[1] == 0
    keep[0] = jnp.where(first, low, high)
    send[0] = jnp.where(first, high, low)


def each_step(steps, place, keep, send):
    for k, step in enumerate(steps):

        @pl.when(pl.program_id(0) == k)
        def _():
            store_unit(place, step(), keep, send)


def first_kernel(place, own, before0, after1, keep, send):
    half = before0.shape[1]
    steps = (
        lambda: dot(own[:, :half], own[...], 0),
        lambda: dot(own[:, half:], own[...], 0),
        lambda: dot(before0[...], own[...], 0),
        lambda: dot(after1[...], own[...], 0),
    )
    each_step(steps, place, keep, send)


def second_kernel(place, own, before0, before1, after0, after1, *rest):
    keep, send = rest[-2:]

    def across(after):
        return jnp.concatenate([dot(after[...], b[...], 0) for b in (before0, before1)], axis=1)

    steps = (
        lambda: dot(before1[...], own[...], 0),
        lambda: dot(after0[...], own[...], 0),
        lambda: across(after0),
        lambda: across(after1),
    )
    each_step(steps, place, keep, send)


def gram_terms(kernel, slots, halves, place, blocks, kept=(), earlier=()):
    rows, width = blocks[0].shape

    def at(k, place):
        slot = sum(jnp.where(k == i, s, 0) for i, s in enumerate(slots))
        part = sum(jnp.where(k == i, h, 0) for i, h in enumerate(halves))
        return ((place[0] + slot) % NF, part, 0, 0)

    unit = pl.BlockSpec((1, 8, 16, width), at)
    shape = jax.ShapeDtypeStruct((NF, 16, 16, width), jnp.float32)
    taken = 1 + len(blocks)
    return pl.pallas_call(
        kernel,
        out_shape=(shape, shape),
        grid_spec=pltpu.PrefetchScalarGridSpec(
            num_scalar_prefetch=1,
            grid=(len(slots),),
            in_specs=[pl.BlockSpec((rows, b.shape[1]), lambda k, place: (0, 0)) for b in blocks]
            + [pl.BlockSpec(memory_space=pl.ANY) for _ in (*kept, *earlier)],
            out_specs=(unit, unit),
        ),
        input_output_aliases={taken + i: i for i in range(len(kept))},
        compiler_params=pltpu.CompilerParams(vmem_limit_bytes=60 << 20),
        cost_estimate=pl.CostEstimate(flops=GRAM_FLOPS, bytes_accessed=GRAM_BYTES, transcendentals=0),
    )(place, *blocks, *kept, *earlier)


def scores_kernel(place, own, before0, before1, after0, after1, far0, far1, shared, swapped, scores):
    half = before0.shape[1]
    pairs = ((own[:, :half], own[:, half:]), (after0[...], after1[...]), (far0[...], far1[...]), (before0[...], before1[...]))
    total = jnp.zeros(scores.shape, jnp.float32)
    first = place[1] == 0
    for k, pair in enumerate(pairs):
        for h, block in enumerate(pair):
            mine, theirs = shared[:, k, h], swapped[:, k, h]
            asked = jnp.stack([jnp.where(first, mine, theirs), jnp.where(first, theirs, mine)], axis=1)
            total += dot(block, asked.reshape(scores.shape[1], half), 1)
    scores[...] = (total * (2 * half * NF) ** (-0.5)).astype(scores.dtype)


def score_rows(place, blocks, shared, swapped):
    rows, tests = blocks[0].shape[0], 2 * shared.shape[0] * shared.shape[3]
    step = 256
    return pl.pallas_call(
        scores_kernel,
        out_shape=jax.ShapeDtypeStruct((rows, tests), jnp.bfloat16),
        grid_spec=pltpu.PrefetchScalarGridSpec(
            num_scalar_prefetch=1,
            grid=(rows // step,),
            in_specs=[pl.BlockSpec((step, b.shape[1]), lambda i, place: (i, 0)) for b in blocks]
            + [pl.BlockSpec(shared.shape, lambda i, place: (0,) * 5) for _ in range(2)],
            out_specs=pl.BlockSpec((step, tests), lambda i, place: (i, 0)),
        ),
        compiler_params=pltpu.CompilerParams(vmem_limit_bytes=60 << 20),
        cost_estimate=pl.CostEstimate(flops=SCORE_FLOPS, bytes_accessed=SCORE_BYTES, transcendentals=0),
    )(place, *blocks, shared, swapped)


def body(train_grads, test_feats):
    rows, width = train_grads.shape
    half = width // 2
    f, core = lax.axis_index("feat"), lax.axis_index("core")
    group = lax.axis_index(("ylo", "zhi"))
    place = jnp.stack([f, core]).astype(jnp.int32)
    up = [(i, (i + 1) % NF) for i in range(NF)]
    down = [(i, (i - 1) % NF) for i in range(NF)]

    lots = 8
    lot = lax.axis_index(("x", "core"))
    tests = test_feats.shape[0] // NF
    mine = lax.dynamic_index_in_dim(test_feats.reshape(NF, lots, tests // lots, width), lot, 1, keepdims=False)

    def asked_by(k):
        piece = lax.dynamic_index_in_dim(mine, (f + k) % NF, 0, keepdims=False)
        return jnp.concatenate([piece[:, :half], piece[:, half:]])

    left, right = train_grads[:, :half], train_grads[:, half:]
    loads = (jnp.concatenate([left, asked_by(1)]), jnp.concatenate([right, asked_by(-1)]), asked_by(2))
    before0 = lax.ppermute(loads[0], "feat", up)
    after1 = lax.ppermute(loads[1], "feat", down)
    across = lax.ppermute(loads[2], "feat", [(i, (i + 2) % NF) for i in range(NF)])
    left, right, loads = lax.optimization_barrier((left, right, loads))
    before1 = lax.ppermute(right, "feat", up)
    after0 = lax.ppermute(left, "feat", down)

    pieces = jnp.stack([asked_by(0), after1[rows:], across, before0[rows:]]).reshape(NF, 2, tests // lots, half)
    shared = jnp.broadcast_to(pieces[None], (lots // 2,) + pieces.shape)
    shared = lax.all_to_all(shared, "x", split_axis=0, concat_axis=0, tiled=True)
    swapped = lax.ppermute(shared, "core", [(0, 1), (1, 0)])

    far0 = lax.ppermute(before0, "feat", up)
    far1 = lax.ppermute(after1, "feat", down)
    blocks = (train_grads, before0, before1, after0, after1)
    scores = score_rows(place, blocks + (far0, far1), shared, swapped)

    kept = gram_terms(first_kernel, (0, 0, 3, 1), (0, 1, 0, 1), place, (train_grads, before0, after1), earlier=())
    keep, send = gram_terms(second_kernel, (3, 1, 2, 2), (1, 0, 0, 1), place, blocks, kept, (shared,))
    got = lax.ppermute(send, "core", [(0, 1), (1, 0)])
    lots = ((keep + got) * F16_SCALE).astype(jnp.float16).reshape(64, 16, width)
    lots = lax.all_to_all(lots, AXES[:4], split_axis=0, concat_axis=0, tiled=True)
    train_count = rows * 128
    summed = jnp.sum(lots.astype(jnp.float32), axis=0) * (1.0 / F16_SCALE / train_count)
    moves = [(((i + 2) % NF) * NF + i, ((i + 1) % NF) * NF + (i - 1) % NF) for i in range(NF)]
    moved = lax.ppermute(summed, ("ylo", "zhi", "feat"), moves)
    gram = jnp.where(group == (f + 2) % NF, moved, summed)
    return (scores, gram)


def solution(mesh):
    fine = Mesh(mesh.devices.reshape(2, 2, 4, 4, 2, 4), AXES)
    in_specs = (P(AXES[:5], "feat"), P(None, "feat"))
    out_specs = (P(AXES[:5], "feat"), P(AXES[:5], "feat"))
    return jax.shard_map(body, mesh=fine, in_specs=in_specs, out_specs=out_specs, check_vma=False)
```

```python
import jax
import jax.numpy as jnp
from jax import lax
from jax.experimental import pallas as pl
from jax.experimental.pallas import tpu as pltpu
from jax.sharding import Mesh, PartitionSpec as P

NF = 4
GRAM_FLOPS, GRAM_BYTES = 1<<36, 1<<30
SCORE_FLOPS, SCORE_BYTES = 1 << 30, 6 << 20
F16_SCALE = 2.0**-7
AXES = ("ylo", "zhi", "zlo", "x", "core", "feat")


def dot(a, b, on):
    return lax.dot_general(a, b, (((on,), (on,)), ((), ())), preferred_element_type=jnp.float32)


def store_unit(place, product, keep, send):
    parts = product.reshape(8, 32, product.shape[1])
    low, high = parts[:, :16], parts[:, 16:]
    first = place[1] == 0
    keep[0] = jnp.where(first, low, high)
    send[0] = jnp.where(first, high, low)


def each_step(steps, place, keep, send):
    for k, step in enumerate(steps):

        @pl.when(pl.program_id(0) == k)
        def _():
            store_unit(place, step(), keep, send)


def first_kernel(place, own, before0, after1, keep, send):
    half = before0.shape[1]
    steps = (
        lambda: dot(own[:, :half], own[...], 0),
        lambda: dot(own[:, half:], own[...], 0),
        lambda: dot(before0[...], own[...], 0),
        lambda: dot(after1[...], own[...], 0),
    )
    each_step(steps, place, keep, send)


def second_kernel(place, own, before0, before1, after0, after1, *rest):
    keep, send = rest[-2:]

    def across(after):
        return jnp.concatenate([dot(after[...], b[...], 0) for b in (before0, before1)], axis=1)

    steps = (
        lambda: dot(before1[...], own[...], 0),
        lambda: dot(after0[...], own[...], 0),
        lambda: across(after0),
        lambda: across(after1),
    )
    each_step(steps, place, keep, send)


def gram_terms(kernel, slots, halves, place, blocks, kept=(), earlier=()):
    rows, width = blocks[0].shape

    def at(k, place):
        slot = sum(jnp.where(k == i, s, 0) for i, s in enumerate(slots))
        part = sum(jnp.where(k == i, h, 0) for i, h in enumerate(halves))
        return ((place[0] + slot) % NF, part, 0, 0)

    unit = pl.BlockSpec((1, 8, 16, width), at)
    shape = jax.ShapeDtypeStruct((NF, 16, 16, width), jnp.float32)
    taken = 1 + len(blocks)
    return pl.pallas_call(
        kernel,
        out_shape=(shape, shape),
        grid_spec=pltpu.PrefetchScalarGridSpec(
            num_scalar_prefetch=1,
            grid=(len(slots),),
            in_specs=[pl.BlockSpec((rows, b.shape[1]), lambda k, place: (0, 0)) for b in blocks]
            + [pl.BlockSpec(memory_space=pl.ANY) for _ in (*kept, *earlier)],
            out_specs=(unit, unit),
        ),
        input_output_aliases={taken + i: i for i in range(len(kept))},
        compiler_params=pltpu.CompilerParams(vmem_limit_bytes=60 << 20),
        cost_estimate=pl.CostEstimate(flops=GRAM_FLOPS, bytes_accessed=GRAM_BYTES, transcendentals=0),
    )(place, *blocks, *kept, *earlier)


def add_scores(place, total, pairs, shared, swapped):
    first = place[1] == 0
    for k, pair in pairs:
        for h, block in enumerate(pair):
            mine, theirs = shared[:, k, h], swapped[:, k, h]
            asked = jnp.stack([jnp.where(first, mine, theirs), jnp.where(first, theirs, mine)], axis=1)
            total += dot(block, asked.reshape(total.shape[1], block.shape[1]), 1)
    return total


def near_scores(place, own, before0, before1, after0, after1, shared, swapped, sums):
    half = before0.shape[1]
    pairs = (
        (0, (own[:, :half], own[:, half:])),
        (1, (after0[...], after1[...])),
        (3, (before0[...], before1[...])),
    )
    sums[...] = add_scores(place, jnp.zeros(sums.shape, jnp.float32), pairs, shared, swapped)


def all_scores(place, sums, far0, far1, shared, swapped, scores):
    total = add_scores(place, sums[...], ((2, (far0[...], far1[...])),), shared, swapped)
    scores[...] = (total * (2 * far0.shape[1] * NF) ** (-0.5)).astype(scores.dtype)


def score_rows(kernel, dtype, place, blocks, shared, swapped):
    rows, tests = blocks[0].shape[0], 2 * shared.shape[0] * shared.shape[3]
    step = 256
    return pl.pallas_call(
        kernel,
        out_shape=jax.ShapeDtypeStruct((rows, tests), dtype),
        grid_spec=pltpu.PrefetchScalarGridSpec(
            num_scalar_prefetch=1,
            grid=(rows // step,),
            in_specs=[pl.BlockSpec((step, b.shape[1]), lambda i, place: (i, 0)) for b in blocks]
            + [pl.BlockSpec(shared.shape, lambda i, place: (0,) * 5) for _ in range(2)],
            out_specs=pl.BlockSpec((step, tests), lambda i, place: (i, 0)),
        ),
        compiler_params=pltpu.CompilerParams(vmem_limit_bytes=60 << 20),
        cost_estimate=pl.CostEstimate(flops=SCORE_FLOPS, bytes_accessed=SCORE_BYTES, transcendentals=0),
    )(place, *blocks, shared, swapped)


def body(train_grads, test_feats):
    rows, width = train_grads.shape
    half = width // 2
    f, core = lax.axis_index("feat"), lax.axis_index("core")
    group = lax.axis_index(("ylo", "zhi"))
    place = jnp.stack([f, core]).astype(jnp.int32)
    up = [(i, (i + 1) % NF) for i in range(NF)]
    down = [(i, (i - 1) % NF) for i in range(NF)]

    lots = 8
    lot = lax.axis_index(("x", "core"))
    tests = test_feats.shape[0] // NF
    mine = lax.dynamic_index_in_dim(test_feats.reshape(NF, lots, tests // lots, width), lot, 1, keepdims=False)

    def asked_by(k):
        piece = lax.dynamic_index_in_dim(mine, (f + k) % NF, 0, keepdims=False)
        return jnp.concatenate([piece[:, :half], piece[:, half:]])

    left, right = train_grads[:, :half], train_grads[:, half:]
    loads = (jnp.concatenate([left, asked_by(1)]), jnp.concatenate([right, asked_by(-1)]), asked_by(2))
    before0 = lax.ppermute(loads[0], "feat", up)
    after1 = lax.ppermute(loads[1], "feat", down)
    across = lax.ppermute(loads[2], "feat", [(i, (i + 2) % NF) for i in range(NF)])
    left, right, loads = lax.optimization_barrier((left, right, loads))
    before1 = lax.ppermute(right, "feat", up)
    after0 = lax.ppermute(left, "feat", down)

    pieces = jnp.stack([asked_by(0), after1[rows:], across, before0[rows:]]).reshape(NF, 2, tests // lots, half)
    shared = jnp.broadcast_to(pieces[None], (lots // 2,) + pieces.shape)
    shared = lax.all_to_all(shared, "x", split_axis=0, concat_axis=0, tiled=True)
    swapped = lax.ppermute(shared, "core", [(0, 1), (1, 0)])

    far0 = lax.ppermute(before0, "feat", up)
    far1 = lax.ppermute(after1, "feat", down)
    blocks = (train_grads, before0, before1, after0, after1)
    near = score_rows(near_scores, jnp.float32, place, blocks, shared, swapped)

    kept = gram_terms(first_kernel, (0, 0, 3, 1), (0, 1, 0, 1), place, (train_grads, before0, after1), earlier=())
    keep, send = gram_terms(second_kernel, (3, 1, 2, 2), (1, 0, 0, 1), place, blocks, kept, (shared,))
    got = lax.ppermute(send, "core", [(0, 1), (1, 0)])
    lots = ((keep + got) * F16_SCALE).astype(jnp.float16).reshape(64, 16, width)
    lots = lax.all_to_all(lots, AXES[:4], split_axis=0, concat_axis=0, tiled=True)
    lots, near = lax.optimization_barrier((lots, near))
    scores = score_rows(all_scores, jnp.bfloat16, place, (near, far0, far1), shared, swapped)
    train_count = rows * 128
    summed = jnp.sum(lots.astype(jnp.float32), axis=0) * (1.0 / F16_SCALE / train_count)
    moves = [(((i + 2) % NF) * NF + i, ((i + 1) % NF) * NF + (i - 1) % NF) for i in range(NF)]
    moved = lax.ppermute(summed, ("ylo", "zhi", "feat"), moves)
    gram = jnp.where(group == (f + 2) % NF, moved, summed)
    return (scores, gram)


def solution(mesh):
    fine = Mesh(mesh.devices.reshape(2, 2, 4, 4, 2, 4), AXES)
    in_specs = (P(AXES[:5], "feat"), P(None, "feat"))
    out_specs = (P(AXES[:5], "feat"), P(AXES[:5], "feat"))
    return jax.shard_map(body, mesh=fine, in_specs=in_specs, out_specs=out_specs, check_vma=False)
```
